768 devices in a mesh: blk: 64 (over x, y, z_hi), rep: 12 (over z_lo, core).
Axes of the slice: x: 4, y: 8, z: 12 (z_hi: 2, z_lo: 6; z = z_hi * 6 + z_lo), core: 2. Of those that a mesh axis runs over, the one named last changes fastest.
Arguments:
- features: bfloat16 [786432, 128], P(('blk', 'rep')), may hold values from -6 to 6
- node_scale: float32 [786432], P(('blk', 'rep')), may hold values from 0.02 to 0.2
- weight: bfloat16 [128, 512], replicated, may hold values from -0.5 to 0.5
- bias: float32 [512], replicated, may hold values from -3 to 3
- cotangent: bfloat16 [786432, 512], P(('blk', 'rep')), may hold values from -0.0068359375 to 0.0068359375
- tile_row: int32 [768, 64], P(('blk', 'rep')), may hold values from 0 to 7
- tile_col: int32 [768, 64], P(('blk', 'rep')), may hold values from 0 to 6143, as said below
- edge_weight: bfloat16 [768, 64, 128, 128], P(('blk', 'rep')), may hold values from 0 to 1
- tile_count: int32 [768], P(('blk', 'rep')), may hold values from 1 to 64, as said below
Outputs:
- hidden: bfloat16 [786432, 512], P(('blk', 'rep'))
- grad_weight: float32 [128, 512], replicated
- grad_bias: float32 [512], replicated
The draws below stay inside these ranges and needn't reach their ends.
Inputs may be any that keep to these rules, and one draw needn't show every extreme that they name: `tile_col`: the column tile of a slot of device d lies in the rows held by loop position d // 12 of blk or by the positions just before or after it on the closed loop of blk. `tile_count`: some device has all 64 slots live.
All inputs are finite; a program needn't handle non-finite values.
Results may differ from the reference program's by a relative error of at most 0.012.
Values may be sent and summed in bfloat16 or wider, within the bound.
A program may use at most 64 MiB of HBM per device.

```python
import math
import jax
import jax.numpy as jnp
from jax import lax

F = 128
H = 512
TILE = 128
BATCH_TILES = 8
TROWS = 8
NT = 64
NODES = 786432
N_BLK = 64
N_REP = 12
DEVICES = 768


def draw_tile_col(key, part):
    key = jax.random.fold_in(key, 7)
    first_key, second_key = jax.random.split(key)
    owner = jnp.arange(DEVICES, dtype=jnp.int32) // N_REP
    offset = jax.random.randint(first_key, (DEVICES, NT), -1, 2, dtype=jnp.int32)
    group_tiles = N_REP * TROWS
    within = jax.random.randint(second_key, (DEVICES, NT), 0, group_tiles, dtype=jnp.int32)
    return (owner[:, None] + offset) % N_BLK * group_tiles + within


def draw_tile_count(key, part):
    key = jax.random.fold_in(key, 11)
    first_key, second_key = jax.random.split(key)
    counts = jax.random.randint(first_key, (DEVICES,), 1, NT + 1, dtype=jnp.int32)
    busiest = jax.random.randint(second_key, (), 0, DEVICES, dtype=jnp.int32)
    return counts.at[busiest].set(NT)


def with_ends(drawn, rng, low, largest):
    longest = drawn.shape.index(max(drawn.shape))
    spots = []
    for shift in (0, 1):
        where = [jax.random.randint(jax.random.fold_in(rng, axis), (), 0, length) for axis, length in enumerate(drawn.shape)]
        where[longest] = (where[longest] + shift) % drawn.shape[longest]
        spots.append(tuple(where))
    return drawn.at[spots[0]].set(low).at[spots[1]].set(largest)


def block_scale(own_key, extent, cuts, smallest, top_value):
    loudness = 1.0
    for position, shards_of in cuts:
        heights = jax.random.uniform(jax.random.fold_in(jax.random.fold_in(own_key, 6), position), (shards_of,), jnp.float32, smallest / len(cuts), top_value / len(cuts))
        loudness = loudness * jnp.repeat(jnp.exp(heights), extent[position] // shards_of).reshape((-1,) + (1,) * (len(extent) - 1 - position))
    return loudness


def centred(key, dims, width, most, cuts=(), kind=jnp.bfloat16):
    entries = width * jax.random.normal(key, dims, jnp.float32)
    if cuts:
        entries = entries * block_scale(key, dims, cuts, -0.22, 0.18)
    return jnp.clip(entries, -most, most).astype(kind)


def setup_inputs(seed: int = 0) -> dict:
    seeds = jax.random.split(jax.random.key(seed), 10)
    return {
        "features": centred(seeds[0], (NODES, F), 1.0, 6.0, ((0, 768),)),
        "node_scale": jnp.clip(jnp.exp(math.log(0.2) - 2.3025851 * jax.random.uniform(seeds[1], (NODES,), jnp.float32) ** block_scale(seeds[1], (NODES,), ((0, 768),), -0.2, 0.2)), 0.02, 0.2),
        "weight": centred(seeds[2], (F, H), F ** -0.5, 0.5),
        "bias": centred(seeds[3], (H,), 0.5, 3.0, (), jnp.float32),
        "cotangent": centred(seeds[4], (NODES, H), NODES ** -0.5, 0.0068359375, ((0, 768),)),
        "tile_row": with_ends(jax.random.randint(seeds[5], (DEVICES, NT), 0, TROWS), jax.random.fold_in(seeds[5], 1), 0, TROWS - 1).astype(jnp.int32),
        "tile_col": draw_tile_col(jax.random.fold_in(seeds[9], 71), 0),
        "edge_weight": jnp.clip(1.0 * jax.random.uniform(seeds[7], (DEVICES, NT, TILE, TILE), jnp.float32) ** block_scale(seeds[7], (DEVICES, NT, TILE, TILE), ((0, 768),), -0.2, 0.2), 0.0, 1.0).astype(jnp.bfloat16),
        "tile_count": draw_tile_count(jax.random.fold_in(seeds[9], 71), 0),
    }


def reference(features, node_scale, weight, bias, cotangent, tile_row, tile_col, edge_weight, tile_count):
    feature_width = features.shape[1]
    scaled = (node_scale[:, None] * features.astype(jnp.float32)).astype(jnp.bfloat16)
    panel_tiles = scaled.reshape(-1, TILE, feature_width)

    def one_device(inputs):
        row_ids, column_ids, device_weights, count_value = inputs

        def step(block_index, running):
            first_slot = (block_index * BATCH_TILES).astype(jnp.int32)
            picked = lax.dynamic_slice_in_dim(column_ids, first_slot, BATCH_TILES)
            panels = jnp.take(panel_tiles, picked, axis=0).astype(jnp.float32)
            tile_values = lax.dynamic_slice_in_dim(device_weights, first_slot, BATCH_TILES).astype(jnp.float32)
            slot_ids = first_slot + jnp.arange(BATCH_TILES, dtype=jnp.int32)
            live_flags = (slot_ids < count_value).astype(jnp.float32)
            edge_values = tile_values * live_flags[:, None, None]
            products = jnp.einsum("kij,kjf->kif", edge_values, panels)
            targets = lax.dynamic_slice_in_dim(row_ids, first_slot, BATCH_TILES)
            onehot = (targets[:, None] == jnp.arange(TROWS, dtype=jnp.int32)[None, :]).astype(jnp.float32)
            return running + jnp.einsum("kr,kif->rif", onehot, products)

        start_value = jnp.zeros((TROWS, TILE, feature_width), jnp.float32)
        return lax.fori_loop(jnp.int32(0), jnp.int32(NT // BATCH_TILES), step, start_value)

    sums = lax.map(one_device, (tile_row, tile_col, edge_weight, tile_count))
    aggregated = (node_scale[:, None] * sums.reshape(-1, feature_width)).astype(jnp.bfloat16)
    preact = jnp.dot(aggregated, weight, preferred_element_type=jnp.float32) + bias
    hidden = jnp.where(preact > 0, preact, jnp.expm1(jnp.minimum(preact, 0.0))).astype(jnp.bfloat16)
    derivative = jnp.where(preact > 0, 1.0, jnp.exp(jnp.minimum(preact, 0.0)))
    grad_pre = (cotangent.astype(jnp.float32) * derivative).astype(jnp.bfloat16)
    grad_weight = lax.dot_general(aggregated, grad_pre, (((0,), (0,)), ((), ())), preferred_element_type=jnp.float32)
    grad_bias = jnp.sum(grad_pre.astype(jnp.float32), axis=0)
    return hidden, grad_weight, grad_bias
```

```python
import functools

import jax
import jax.numpy as jnp
from jax import lax
from jax.experimental import pallas as pl
from jax.experimental.pallas import tpu as pltpu
from jax.sharding import PartitionSpec as P

TILE = 128
BATCH = 8
PARTS = 4
SKEW = 2
LAG = 3
MESH = pl.DeviceIdType.MESH
VMEM_LIMIT = 48 * 1024 * 1024


def spread(row):
    return jnp.transpose(jnp.broadcast_to(row, (TILE, TILE)))


def place(columns, half):
    blk, rep = lax.axis_index("blk"), lax.axis_index("rep")
    upper = lax.rem(blk, 2)
    core = lax.rem(rep, 2)
    chip = upper * half + lax.div(rep, 2)
    return blk, rep, lax.div(blk, 2), upper, chip, core


def greet(partners):
    barrier = pltpu.get_barrier_semaphore()
    for partner in partners:
        pl.semaphore_signal(barrier, inc=1, device_id=partner, device_id_type=MESH)
    pl.semaphore_wait(barrier, len(partners))


def gather_kernel(
    columns, half, features, scale, out, mine, ring_recv, side_recv, mate_recv, ring_sent, side_sent, mate_sent, kept
):
    chips = 2 * half
    rows = features.shape[0]
    part = rows // PARTS
    blk, rep, column, upper, chip, core = place(columns, half)
    way = 1 - 2 * core

    def chip_id(c):
        return (2 * column + lax.div(c, half), 2 * lax.rem(c, half) + core)

    def around(steps):
        return lax.rem(chip + way * steps + 2 * chips, chips)

    ahead, behind = chip_id(around(1)), chip_id(around(-1))
    turn = 1 - 2 * upper
    side_to = (2 * lax.rem(column + turn + columns, columns) + upper, rep)
    side_from = (2 * lax.rem(column - turn + columns, columns) + upper, rep)
    mate = (blk, rep + way)
    greet((ahead, behind, side_to, side_from, mate))

    for t in range(rows // TILE):
        span = pl.ds(t * TILE, TILE)
        mine[span, :] = (spread(scale[pl.ds(t, 1), :]) * features[span, :].astype(jnp.float32)).astype(mine.dtype)
    own = 2 * chip + core
    keep = pltpu.make_async_copy(mine, out.at[own], kept)
    keep.start()

    def chunk(q):
        return pl.ds(pl.multiple_of(q * part, part), part)

    def ring(direction, step, q, source, piece, target):
        return pltpu.make_async_remote_copy(
            src_ref=source,
            dst_ref=out.at[piece, chunk(q)],
            send_sem=ring_sent,
            recv_sem=ring_recv.at[(direction * half + step) * PARTS + q],
            device_id=target,
            device_id_type=MESH,
        )

    def side(direction, step, q, piece):
        return pltpu.make_async_remote_copy(
            src_ref=out.at[piece, chunk(q)],
            dst_ref=out.at[2 * chips + lax.rem(piece, 2 * half), chunk(q)],
            send_sem=side_sent,
            recv_sem=side_recv.at[(direction * half + step) * PARTS + q],
            device_id=side_to,
            device_id_type=MESH,
        )

    def share(source, piece, q):
        pltpu.make_async_remote_copy(
            src_ref=source,
            dst_ref=out.at[piece, chunk(q)],
            send_sem=mate_sent,
            recv_sem=mate_recv,
            device_id=mate,
            device_id_type=MESH,
        ).start()

    lengths = (half, half - 1)
    targets = (ahead, behind)

    def arrived(direction, step):
        c = around(-step if direction == 0 else step)
        return 2 * c + core, lax.div(c, half) != upper

    def tick(time, _):
        def each(q, _):
            step = time - SKEW * q

            @pl.when(step == 0)
            def _():
                source = mine.at[chunk(q)]
                ring(0, 0, q, source, own, ahead).start()
                ring(1, 0, q, source, own, behind).start()
                share(source, own, q)

            for direction in range(2):

                @pl.when((step >= 1) & (step <= lengths[direction]))
                def _():
                    piece, foreign = arrived(direction, step)
                    here = out.at[piece, chunk(q)]
                    ring(direction, step - 1, q, here, piece, targets[direction]).wait_recv()

                    @pl.when(step < lengths[direction])
                    def _():
                        ring(direction, step, q, here, piece, targets[direction]).start()

                    @pl.when(foreign)
                    def _():
                        side(direction, step - 1, q, piece).start()

                    share(here, piece, q)

            late = step - LAG
            for direction in range(2):

                @pl.when((late >= 1) & (late <= lengths[direction]))
                def _():
                    piece, foreign = arrived(direction, late)

                    @pl.when(foreign)
                    def _():
                        side(direction, late - 1, q, piece).wait_recv()
                        third = 2 * chips + lax.rem(piece, 2 * half)
                        share(out.at[third, chunk(q)], third, q)

            return 0

        return lax.fori_loop(0, PARTS, each, 0)

    lax.fori_loop(0, half + SKEW * (PARTS - 1) + LAG + 1, tick, 0)

    def drain(pieces, semaphore):
        span = out.at[pl.ds(0, pieces)]
        pltpu.make_async_copy(span, span, semaphore).wait()

    keep.wait()
    drain(chips - 1, ring_sent)
    drain(half, side_sent)
    drain(chips + half, mate_sent)
    drain(chips + half, mate_recv)


def layer_kernel(
    half, tile_row, tile_col, tile_count, panels, edges, scale, weight, bias, cotangent, hidden, grad, grad_bias,
    picked, values, upstream, total, slot_sem, value_sem, up_sem,
):
    slots = edges.shape[0]
    rows = total.shape[0]
    width = weight.shape[1]
    blk = lax.axis_index("blk")
    blks = lax.axis_size("blk")
    upper = lax.rem(blk, 2)
    live = tile_count[0]
    batches = lax.div(live + (BATCH - 1), BATCH)
    tiles = rows // TILE
    group_tiles = 2 * half * tiles

    cotangent_copy = pltpu.make_async_copy(cotangent, upstream, up_sem)

    def values_copy(b):
        span = pl.ds(b * BATCH, BATCH)
        return pltpu.make_async_copy(edges.at[span], values.at[span], value_sem.at[b])

    def fetch(b, _):
        values_copy(b).start()
        for i in range(BATCH):
            k = b * BATCH + i
            col = tile_col[0, k]
            position = lax.div(col, group_tiles)
            offset = lax.rem(position - blk + blks, blks)
            part = jnp.where(offset == 0, upper, jnp.where(offset == jnp.where(upper == 0, 1, blks - 1), 1 - upper, 2))
            tile = part * group_tiles + lax.rem(col, group_tiles)
            pltpu.make_async_copy(panels.at[tile], picked.at[k], slot_sem.at[b]).start()
        return 0

    lax.fori_loop(0, batches, fetch, 0)
    cotangent_copy.start()
    total[...] = jnp.zeros_like(total)

    def multiply(b, _):
        values_copy(b).wait()
        span = pl.ds(b * BATCH, BATCH)
        pltpu.make_async_copy(picked.at[span], picked.at[span], slot_sem.at[b]).wait()
        products = []
        for i in range(BATCH):
            k = b * BATCH + i
            product = jnp.dot(values[k], picked[k], preferred_element_type=jnp.float32)
            products.append(jnp.where(k < live, product, 0.0))
        for i in range(BATCH):
            start = pl.multiple_of(tile_row[0, b * BATCH + i] * TILE, TILE)
            total[pl.ds(start, TILE), :] += products[i]
        return 0

    lax.fori_loop(0, batches, multiply, 0)
    cotangent_copy.wait()
    grad_total = jnp.zeros((TILE, width), jnp.float32)
    bias_total = jnp.zeros((8, width), jnp.float32)
    for t in range(tiles):
        span = pl.ds(t * TILE, TILE)
        aggregated = (spread(scale[pl.ds(t, 1), :]) * total[span, :]).astype(jnp.bfloat16)
        preact = jnp.dot(aggregated, weight[...], preferred_element_type=jnp.float32) + bias[...]
        positive = preact > 0
        power = jnp.exp(jnp.minimum(preact, 0.0))
        hidden[span, :] = jnp.where(positive, preact, power - 1.0).astype(hidden.dtype)
        grad_pre = (upstream[span, :].astype(jnp.float32) * jnp.where(positive, 1.0, power)).astype(jnp.bfloat16)
        grad_total += lax.dot_general(
            aggregated, grad_pre, (((0,), (0,)), ((), ())), preferred_element_type=jnp.float32
        )
        bias_total += jnp.sum(grad_pre.astype(jnp.float32).reshape(TILE // 8, 8, width), axis=0)
    lanes = width // TILE
    for i in range(TILE // 8):
        for j in range(lanes):
            grad[i * lanes + j] = grad_total[8 * i : 8 * i + 8, TILE * j : TILE * (j + 1)]
    bias_row = jnp.sum(bias_total, axis=0, keepdims=True)
    grad_bias[...] = jnp.zeros_like(grad_bias)
    for j in range(lanes):
        grad_bias[j : j + 1, :] = bias_row[:, TILE * j : TILE * (j + 1)]


def sum_kernel(
    columns, half, grad, grad_bias, out, out_bias,
    from_mate, bias_mate, message, inbox, line, full,
    mate_recv, bias_recv, plane_recv, line_recv, back_recv, last_recv,
    mate_sent, bias_sent, plane_sent, line_sent, back_sent, last_sent,
):
    chips = 2 * half
    blk, rep, column, upper, chip, core = place(columns, half)
    share = grad.shape[0] // 2 // columns
    mate = (blk, rep + 1 - 2 * core)

    def plane_id(j):
        return (2 * j + upper, rep)

    def line_id(c):
        return (2 * column + lax.div(c, half), 2 * lax.rem(c, half) + core)

    barrier = pltpu.get_barrier_semaphore()

    def greet_plane(o, _):
        pl.semaphore_signal(barrier, inc=1, device_id=plane_id(lax.rem(column + o, columns)), device_id_type=MESH)
        return 0

    def greet_line(o, _):
        pl.semaphore_signal(barrier, inc=1, device_id=line_id(lax.rem(chip + o, chips)), device_id_type=MESH)
        return 0

    pl.semaphore_signal(barrier, inc=1, device_id=mate, device_id_type=MESH)
    lax.fori_loop(1, columns, greet_plane, 0)
    lax.fori_loop(1, chips, greet_line, 0)
    pl.semaphore_wait(barrier, columns + chips - 1)

    count = columns * share

    def remote(source, target, sent, received, device):
        return pltpu.make_async_remote_copy(
            src_ref=source, dst_ref=target, send_sem=sent, recv_sem=received, device_id=device, device_id_type=MESH
        )

    other = remote(grad.at[pl.ds((1 - core) * count, count)], from_mate, mate_sent, mate_recv, mate)
    other.start()
    other_bias = remote(grad_bias, bias_mate, bias_sent, bias_recv, mate)
    other_bias.start()
    other_bias.wait()
    bias_sum = grad_bias[...] + bias_mate[...]
    other.wait()
    for j in range(columns):
        for i in range(share):
            message[j, 8 * i : 8 * i + 8, :] = grad[core * count + j * share + i] + from_mate[j * share + i]
        message[j, 8 * share :, :] = bias_sum

    def send_plane(o, _):
        j = lax.rem(column + o, columns)
        remote(message.at[j], inbox.at[column], plane_sent, plane_recv, plane_id(j)).start()
        return 0

    lax.fori_loop(1, columns, send_plane, 0)
    inbox[column] = message[column]
    pltpu.make_async_copy(inbox.at[pl.ds(1, columns - 1)], inbox.at[pl.ds(1, columns - 1)], plane_recv).wait()
    line[chip] = jnp.sum(inbox[...], axis=0)

    def send_line(o, _):
        c = lax.rem(chip + o, chips)
        remote(line.at[chip], line.at[chip], line_sent, line_recv, line_id(c)).start()
        return 0

    lax.fori_loop(1, chips, send_line, 0)
    pltpu.make_async_copy(line.at[pl.ds(1, chips - 1)], line.at[pl.ds(1, chips - 1)], line_recv).wait()
    final = jnp.sum(line[...], axis=0)
    base = core * columns + column
    for i in range(share):
        full[base, i] = final[8 * i : 8 * i + 8, :]
    out_bias[...] = final[8 * share :, :]

    def send_back(o, _):
        j = lax.rem(column + o, columns)
        remote(full.at[base], full.at[base], back_sent, back_recv, plane_id(j)).start()
        return 0

    lax.fori_loop(1, columns, send_back, 0)
    pltpu.make_async_copy(full.at[pl.ds(1, columns - 1)], full.at[pl.ds(1, columns - 1)], back_recv).wait()
    mine = full.at[pl.ds(core * columns, columns)]
    last = remote(mine, mine, last_sent, last_recv, mate)
    last.start()
    last.wait()
    lanes = out.shape[1] // TILE
    for j in range(2 * columns):
        for i in range(share):
            n = j * share + i
            r, c = divmod(n, lanes)
            out[8 * r : 8 * r + 8, TILE * c : TILE * (c + 1)] = full[j, i]
    pltpu.make_async_copy(message.at[pl.ds(1, columns - 1)], message.at[pl.ds(1, columns - 1)], plane_sent).wait()
    pltpu.make_async_copy(line.at[pl.ds(1, chips - 1)], line.at[pl.ds(1, chips - 1)], line_sent).wait()
    pltpu.make_async_copy(full.at[pl.ds(1, columns - 1)], full.at[pl.ds(1, columns - 1)], back_sent).wait()


def shards(features, node_scale, weight, bias, cotangent, tile_row, tile_col, edge_weight, tile_count):
    rows, depth = features.shape
    width = weight.shape[1]
    slots = tile_col.shape[1]
    columns = lax.axis_size("blk") // 2
    half = lax.axis_size("rep") // 2
    chips = 2 * half
    pieces = 2 * chips + 2 * half
    scale = node_scale.reshape(rows // TILE, TILE)
    vmem = pl.BlockSpec(memory_space=pltpu.VMEM)
    smem = pl.BlockSpec(memory_space=pltpu.SMEM)
    hbm = pl.BlockSpec(memory_space=pl.ANY)
    dma = pltpu.SemaphoreType.DMA

    gathered = pl.pallas_call(
        functools.partial(gather_kernel, columns, half),
        name="gather",
        out_shape=jax.ShapeDtypeStruct((pieces, rows, depth), jnp.bfloat16),
        in_specs=[vmem, vmem],
        out_specs=hbm,
        scratch_shapes=[
            pltpu.VMEM((rows, depth), jnp.bfloat16),
            dma((2 * half * PARTS,)),
            dma((2 * half * PARTS,)),
            dma(()),
            dma(()),
            dma(()),
            dma(()),
            dma(()),
        ],
        compiler_params=pltpu.CompilerParams(
            collective_id=0, has_side_effects=True, vmem_limit_bytes=VMEM_LIMIT
        ),
    )(features, scale)

    chunks = TILE * width // (8 * TILE)
    hidden, grad, grad_bias = pl.pallas_call(
        functools.partial(layer_kernel, half),
        name="layer",
        out_shape=(
            jax.ShapeDtypeStruct((rows, width), jnp.bfloat16),
            jax.ShapeDtypeStruct((chunks, 8, TILE), jnp.float32),
            jax.ShapeDtypeStruct((8, TILE), jnp.float32),
        ),
        in_specs=[smem, smem, smem, hbm, hbm, vmem, vmem, vmem, hbm],
        out_specs=(vmem, vmem, vmem),
        scratch_shapes=[
            pltpu.VMEM((slots, TILE, depth), jnp.bfloat16),
            pltpu.VMEM((slots, TILE, TILE), jnp.bfloat16),
            pltpu.VMEM((rows, width), jnp.bfloat16),
            pltpu.VMEM((rows, depth), jnp.float32),
            dma((slots // BATCH,)),
            dma((slots // BATCH,)),
            dma(()),
        ],
        compiler_params=pltpu.CompilerParams(vmem_limit_bytes=VMEM_LIMIT),
    )(
        tile_row, tile_col, tile_count, gathered.reshape(-1, TILE, depth), edge_weight[0], scale, weight,
        bias.reshape(1, width), cotangent,
    )

    share = chunks // 2 // columns
    tall = 8 * share + 8
    grad_weight, bias_sum = pl.pallas_call(
        functools.partial(sum_kernel, columns, half),
        name="sum",
        out_shape=(
            jax.ShapeDtypeStruct((TILE, width), jnp.float32),
            jax.ShapeDtypeStruct((8, TILE), jnp.float32),
        ),
        in_specs=[vmem, vmem],
        out_specs=(vmem, vmem),
        scratch_shapes=[
            pltpu.VMEM((chunks // 2, 8, TILE), jnp.float32),
            pltpu.VMEM((8, TILE), jnp.float32),
            pltpu.VMEM((columns, tall, TILE), jnp.float32),
            pltpu.VMEM((columns, tall, TILE), jnp.float32),
            pltpu.VMEM((chips, tall, TILE), jnp.float32),
            pltpu.VMEM((2 * columns, share, 8, TILE), jnp.float32),
        ]
        + [dma(())] * 12,
        compiler_params=pltpu.CompilerParams(
            collective_id=1, has_side_effects=True, vmem_limit_bytes=VMEM_LIMIT
        ),
    )(grad, grad_bias)
    return hidden, grad_weight, bias_sum.reshape(-1)[:width]


def solution(mesh):
    rows = P(("blk", "rep"))
    in_specs = (
        P(("blk", "rep"), None),
        rows,
        P(),
        P(),
        P(("blk", "rep"), None),
        P(("blk", "rep"), None),
        P(("blk", "rep"), None),
        P(("blk", "rep"), None, None, None),
        rows,
    )
    out_specs = (P(("blk", "rep"), None), P(), P())
    return jax.shard_map(shards, mesh=mesh, in_specs=in_specs, out_specs=out_specs, check_vma=False)
```

```python
import functools

import jax
import jax.numpy as jnp
from jax import lax
from jax.experimental import pallas as pl
from jax.experimental.pallas import tpu as pltpu
from jax.sharding import PartitionSpec as P

TILE = 128
BATCH = 8
PARTS = 4
SKEW = 0
LAG = 3
WIRE = jnp.bfloat16
ACROSS = 8
MESH = pl.DeviceIdType.MESH
VMEM_LIMIT = 24 * 1024 * 1024


def spread(row):
    return jnp.transpose(jnp.broadcast_to(row, (TILE, TILE)))


def place(columns, half):
    blk, rep = lax.axis_index("blk"), lax.axis_index("rep")
    upper = lax.rem(blk, 2)
    core = lax.rem(rep, 2)
    chip = upper * half + lax.div(rep, 2)
    return blk, rep, lax.div(blk, 2), upper, chip, core


def gather_kernel(
    columns, half, features, scale, out, mine, ring_recv, side_recv, mate_recv, ring_sent, side_sent, mate_sent, kept
):
    chips = 2 * half
    rows = features.shape[0]
    part = rows // PARTS
    blk, rep, column, upper, chip, core = place(columns, half)
    way = 1 - 2 * core

    def chip_id(c):
        return (2 * column + lax.div(c, half), 2 * lax.rem(c, half) + core)

    def around(steps):
        return lax.rem(chip + way * steps + 2 * chips, chips)

    ahead, behind = chip_id(around(1)), chip_id(around(-1))
    turn = 1 - 2 * upper
    side_to = (2 * lax.rem(column + turn + columns, columns) + upper, rep)
    side_from = (2 * lax.rem(column - turn + columns, columns) + upper, rep)
    mate = (blk, rep + way)
    partners = (ahead, behind, side_to, side_from, mate)
    barrier = pltpu.get_barrier_semaphore()
    for partner in partners:
        pl.semaphore_signal(barrier, inc=1, device_id=partner, device_id_type=MESH)

    for t in range(rows // TILE):
        span = pl.ds(t * TILE, TILE)
        mine[span, :] = (spread(scale[pl.ds(t, 1), :]) * features[span, :].astype(jnp.float32)).astype(mine.dtype)
    pl.semaphore_wait(barrier, len(partners))
    own = 2 * chip + core
    keep = pltpu.make_async_copy(mine, out.at[own], kept)
    keep.start()

    def chunk(q):
        return pl.ds(pl.multiple_of(q * part, part), part)

    def ring(direction, step, q, source, piece, target):
        return pltpu.make_async_remote_copy(
            src_ref=source,
            dst_ref=out.at[piece, chunk(q)],
            send_sem=ring_sent,
            recv_sem=ring_recv.at[(direction * half + step) * PARTS + q],
            device_id=target,
            device_id_type=MESH,
        )

    def side(direction, step, q, piece):
        return pltpu.make_async_remote_copy(
            src_ref=out.at[piece, chunk(q)],
            dst_ref=out.at[2 * chips + lax.rem(piece, 2 * half), chunk(q)],
            send_sem=side_sent,
            recv_sem=side_recv.at[(direction * half + step) * PARTS + q],
            device_id=side_to,
            device_id_type=MESH,
        )

    def share(source, piece, q):
        pltpu.make_async_remote_copy(
            src_ref=source,
            dst_ref=out.at[piece, chunk(q)],
            send_sem=mate_sent,
            recv_sem=mate_recv,
            device_id=mate,
            device_id_type=MESH,
        ).start()

    lengths = (half, half - 1)
    targets = (ahead, behind)

    def arrived(direction, step):
        c = around(-step if direction == 0 else step)
        return 2 * c + core, lax.div(c, half) != upper

    def tick(time, _):
        def each(q, _):
            step = time - SKEW * q

            @pl.when(step == 0)
            def _():
                source = mine.at[chunk(q)]
                ring(0, 0, q, source, own, ahead).start()
                ring(1, 0, q, source, own, behind).start()
                share(source, own, q)

            for direction in range(2):

                @pl.when((step >= 1) & (step <= lengths[direction]))
                def _():
                    piece, foreign = arrived(direction, step)
                    here = out.at[piece, chunk(q)]
                    ring(direction, step - 1, q, here, piece, targets[direction]).wait_recv()

                    @pl.when(step < lengths[direction])
                    def _():
                        ring(direction, step, q, here, piece, targets[direction]).start()

                    @pl.when(foreign)
                    def _():
                        side(direction, step - 1, q, piece).start()

                    share(here, piece, q)

            late = step - LAG
            for direction in range(2):

                @pl.when((late >= 1) & (late <= lengths[direction]))
                def _():
                    piece, foreign = arrived(direction, late)

                    @pl.when(foreign)
                    def _():
                        side(direction, late - 1, q, piece).wait_recv()
                        third = 2 * chips + lax.rem(piece, 2 * half)
                        share(out.at[third, chunk(q)], third, q)

            return 0

        return lax.fori_loop(0, PARTS, each, 0)

    lax.fori_loop(0, half + SKEW * (PARTS - 1) + LAG + 1, tick, 0)

    def drain(pieces, semaphore):
        span = out.at[pl.ds(0, pieces)]
        pltpu.make_async_copy(span, span, semaphore).wait()

    keep.wait()
    drain(chips - 1, ring_sent)
    drain(half, side_sent)
    drain(chips + half, mate_sent)
    drain(chips + half, mate_recv)


def layer_kernel(
    half, tile_row, tile_col, tile_count, panels, edges, scale, weight, bias, cotangent, hidden, summed, upstream, total
):
    rows = total.shape[0]
    blk = lax.axis_index("blk")
    blks = lax.axis_size("blk")
    upper = lax.rem(blk, 2)
    live = tile_count[0]
    tiles = rows // TILE
    group_tiles = 2 * half * tiles
    total[...] = jnp.zeros_like(total)

    def multiply(b, _):
        products = []
        for i in range(BATCH):
            k = b * BATCH + i
            col = tile_col[0, k]
            position = lax.div(col, group_tiles)
            offset = lax.rem(position - blk + blks, blks)
            part = jnp.where(offset == 0, upper, jnp.where(offset == jnp.where(upper == 0, 1, blks - 1), 1 - upper, 2))
            tile = part * group_tiles + lax.rem(col, group_tiles)
            product = jnp.dot(edges[k], panels[tile], preferred_element_type=jnp.float32)
            products.append(jnp.where(k < live, product, 0.0))
        for i in range(BATCH):
            start = pl.multiple_of(tile_row[0, b * BATCH + i] * TILE, TILE)
            total[pl.ds(start, TILE), :] += products[i]
        return 0

    lax.fori_loop(0, lax.div(live + (BATCH - 1), BATCH), multiply, 0)
    for t in range(tiles):
        span = pl.ds(t * TILE, TILE)
        aggregated = (spread(scale[pl.ds(t, 1), :]) * total[span, :]).astype(jnp.bfloat16)
        summed[span, :] = aggregated
        preact = jnp.dot(aggregated, weight[...], preferred_element_type=jnp.float32) + bias[...]
        positive = preact > 0
        power = jnp.exp(jnp.minimum(preact, 0.0))
        hidden[span, :] = jnp.where(positive, preact, power - 1.0).astype(hidden.dtype)
        slope = jnp.where(positive, 1.0, power)
        upstream[span, :] = (cotangent[span, :].astype(jnp.float32) * slope).astype(upstream.dtype)


def farthest(t, size):
    step = lax.div(t + 1, 2)
    return size // 2 + jnp.where(lax.rem(t, 2) == 0, step, -step)


def sum_kernel(
    columns, half, summed, upstream, out, out_bias,
    grad, grad_bias, from_mate, bias_mate, message, inbox, line, full,
    mate_recv, bias_recv, plane_recv, line_recv, back_recv, last_recv,
    mate_sent, bias_sent, plane_sent, line_sent, back_sent, last_sent,
):
    chips = 2 * half
    blk, rep, column, upper, chip, core = place(columns, half)
    mate = (blk, rep + 1 - 2 * core)
    x, y = lax.div(column, ACROSS), lax.rem(column, ACROSS)
    deep = columns // ACROSS
    lanes = out.shape[1] // TILE

    def each_plane(act):
        def body(e, _):
            to_x = lax.rem(x + farthest(lax.div(e, ACROSS), deep), deep)
            to_y = lax.rem(y + farthest(lax.rem(e, ACROSS), ACROSS), ACROSS)
            j = to_x * ACROSS + to_y
            act((2 * j + upper, rep), j)
            return 0

        lax.fori_loop(0, columns - 1, body, 0)

    def each_line(act):
        def body(e, _):
            c = lax.rem(chip + farthest(e, chips), chips)
            act((2 * column + lax.div(c, half), 2 * lax.rem(c, half) + core))
            return 0

        lax.fori_loop(0, chips - 1, body, 0)

    barrier = pltpu.get_barrier_semaphore()
    each_line(lambda device: pl.semaphore_signal(barrier, inc=1, device_id=device, device_id_type=MESH))
    each_plane(lambda device, j: pl.semaphore_signal(barrier, inc=1, device_id=device, device_id_type=MESH))
    pl.semaphore_signal(barrier, inc=1, device_id=mate, device_id_type=MESH)

    weight_part = lax.dot_general(
        summed[...], upstream[...], (((0,), (0,)), ((), ())), preferred_element_type=jnp.float32
    )
    bias_part = jnp.sum(upstream[...].astype(jnp.float32), axis=0, keepdims=True)
    for c in range(2):
        for j in range(columns):
            r, s = divmod(c * columns + j, lanes)
            grad[c, j] = weight_part[8 * r : 8 * r + 8, TILE * s : TILE * (s + 1)]
    grad_bias[...] = jnp.zeros_like(grad_bias)
    for s in range(lanes):
        grad_bias[s : s + 1, :] = bias_part[:, TILE * s : TILE * (s + 1)]
    pl.semaphore_wait(barrier, columns + chips - 1)

    def remote(source, target, sent, received, device):
        return pltpu.make_async_remote_copy(
            src_ref=source, dst_ref=target, send_sem=sent, recv_sem=received, device_id=device, device_id_type=MESH
        )

    def landed(buffer, pieces, semaphore):
        span = buffer.at[pl.ds(0, pieces)]
        pltpu.make_async_copy(span, span, semaphore).wait()

    other = remote(grad.at[1 - core], from_mate, mate_sent, mate_recv, mate)
    other.start()
    other_bias = remote(grad_bias, bias_mate, bias_sent, bias_recv, mate)
    other_bias.start()
    other_bias.wait()
    bias_sum = grad_bias[...] + bias_mate[...]
    other.wait()
    for j in range(columns):
        message[j] = jnp.concatenate([grad[core, j] + from_mate[j], bias_sum], axis=0).astype(message.dtype)

    each_plane(lambda device, j: remote(message.at[j], inbox.at[column], plane_sent, plane_recv, device).start())
    inbox[column] = message[column]
    landed(inbox, columns - 1, plane_recv)
    line[chip] = jnp.sum(inbox[...].astype(jnp.float32), axis=0).astype(line.dtype)

    each_line(lambda device: remote(line.at[chip], line.at[chip], line_sent, line_recv, device).start())
    landed(line, chips - 1, line_recv)
    final = jnp.sum(line[...].astype(jnp.float32), axis=0)
    full[core, column] = final[0:8, :]
    out_bias[...] = final[8:16, :]

    here = full.at[core, column]
    each_plane(lambda device, j: remote(here, here, back_sent, back_recv, device).start())
    landed(full.at[core], columns - 1, back_recv)
    mine = full.at[core]
    last = remote(mine, mine, last_sent, last_recv, mate)
    last.start()
    last.wait()
    for c in range(2):
        for j in range(columns):
            r, s = divmod(c * columns + j, lanes)
            out[8 * r : 8 * r + 8, TILE * s : TILE * (s + 1)] = full[c, j]
    landed(message, columns - 1, plane_sent)
    landed(line, chips - 1, line_sent)
    landed(full.at[core], columns - 1, back_sent)


def shards(features, node_scale, weight, bias, cotangent, tile_row, tile_col, edge_weight, tile_count):
    rows, depth = features.shape
    width = weight.shape[1]
    columns = lax.axis_size("blk") // 2
    half = lax.axis_size("rep") // 2
    chips = 2 * half
    pieces = 2 * chips + 2 * half
    scale = node_scale.reshape(rows // TILE, TILE)
    vmem = pl.BlockSpec(memory_space=pltpu.VMEM)
    smem = pl.BlockSpec(memory_space=pltpu.SMEM)
    dma = pltpu.SemaphoreType.DMA

    gathered = pl.pallas_call(
        functools.partial(gather_kernel, columns, half),
        name="gather",
        out_shape=jax.ShapeDtypeStruct((pieces, rows, depth), jnp.bfloat16),
        in_specs=[vmem, vmem],
        out_specs=vmem,
        scratch_shapes=[
            pltpu.VMEM((rows, depth), jnp.bfloat16),
            dma((2 * half * PARTS,)),
            dma((2 * half * PARTS,)),
        ]
        + [dma(())] * 5,
        compiler_params=pltpu.CompilerParams(
            collective_id=0, has_side_effects=True, vmem_limit_bytes=VMEM_LIMIT
        ),
    )(features, scale)

    hidden, summed, upstream = pl.pallas_call(
        functools.partial(layer_kernel, half),
        name="layer",
        out_shape=(
            jax.ShapeDtypeStruct((rows, width), jnp.bfloat16),
            jax.ShapeDtypeStruct((rows, depth), jnp.bfloat16),
            jax.ShapeDtypeStruct((rows, width), jnp.bfloat16),
        ),
        in_specs=[smem] * 3 + [vmem] * 6,
        out_specs=(vmem, vmem, vmem),
        scratch_shapes=[pltpu.VMEM((rows, depth), jnp.float32)],
        compiler_params=pltpu.CompilerParams(vmem_limit_bytes=VMEM_LIMIT),
    )(
        tile_row, tile_col, tile_count, gathered.reshape(-1, TILE, depth), edge_weight[0], scale, weight,
        bias.reshape(1, width), cotangent,
    )

    grad_weight, bias_sum = pl.pallas_call(
        functools.partial(sum_kernel, columns, half),
        name="sum",
        out_shape=(
            jax.ShapeDtypeStruct((depth, width), jnp.float32),
            jax.ShapeDtypeStruct((8, TILE), jnp.float32),
        ),
        in_specs=[vmem, vmem],
        out_specs=(vmem, vmem),
        scratch_shapes=[
            pltpu.VMEM((2, columns, 8, TILE), jnp.float32),
            pltpu.VMEM((8, TILE), jnp.float32),
            pltpu.VMEM((columns, 8, TILE), jnp.float32),
            pltpu.VMEM((8, TILE), jnp.float32),
            pltpu.VMEM((columns, 16, TILE), WIRE),
            pltpu.VMEM((columns, 16, TILE), WIRE),
            pltpu.VMEM((chips, 16, TILE), WIRE),
            pltpu.VMEM((2, columns, 8, TILE), jnp.float32),
        ]
        + [dma(())] * 12,
        compiler_params=pltpu.CompilerParams(
            collective_id=1, has_side_effects=True, vmem_limit_bytes=VMEM_LIMIT
        ),
    )(summed, upstream)
    return hidden, grad_weight, bias_sum.reshape(-1)[:width]


def solution(mesh):
    rows = P(("blk", "rep"))
    in_specs = (
        P(("blk", "rep"), None),
        rows,
        P(),
        P(),
        P(("blk", "rep"), None),
        P(("blk", "rep"), None),
        P(("blk", "rep"), None),
        P(("blk", "rep"), None, None, None),
        rows,
    )
    out_specs = (P(("blk", "rep"), None), P(), P())
    return jax.shard_map(shards, mesh=mesh, in_specs=in_specs, out_specs=out_specs, check_vma=False)
```

```python
import functools

import jax
import jax.numpy as jnp
from jax import lax
from jax.experimental import pallas as pl
from jax.experimental.pallas import tpu as pltpu
from jax.sharding import PartitionSpec as P

TILE = 128
BATCH = 8
PARTS = 4
SKEW = 0
LAG = 3
WIRE = jnp.bfloat16
ACROSS = 8
MESH = pl.DeviceIdType.MESH
VMEM_LIMIT = 24 * 1024 * 1024


def spread(row):
    return jnp.transpose(jnp.broadcast_to(row, (TILE, TILE)))


def place(columns, half):
    blk, rep = lax.axis_index("blk"), lax.axis_index("rep")
    upper = lax.rem(blk, 2)
    core = lax.rem(rep, 2)
    chip = upper * half + lax.div(rep, 2)
    return blk, rep, lax.div(blk, 2), upper, chip, core


def gather_kernel(
    columns, half, features, scale, out, mine, ring_recv, side_recv, mate_recv, ring_sent, side_sent, mate_sent, kept
):
    chips = 2 * half
    rows = features.shape[0]
    part = rows // PARTS
    blk, rep, column, upper, chip, core = place(columns, half)
    way = 1 - 2 * core

    def chip_id(c):
        return (2 * column + lax.div(c, half), 2 * lax.rem(c, half) + core)

    def around(steps):
        return lax.rem(chip + way * steps + 2 * chips, chips)

    ahead, behind = chip_id(around(1)), chip_id(around(-1))
    turn = 1 - 2 * upper
    side_to = (2 * lax.rem(column + turn + columns, columns) + upper, rep)
    side_from = (2 * lax.rem(column - turn + columns, columns) + upper, rep)
    mate = (blk, rep + way)
    partners = (ahead, behind, side_to, side_from, mate)
    barrier = pltpu.get_barrier_semaphore()
    for partner in partners:
        pl.semaphore_signal(barrier, inc=1, device_id=partner, device_id_type=MESH)

    for t in range(rows // TILE):
        span = pl.ds(t * TILE, TILE)
        mine[span, :] = (spread(scale[pl.ds(t, 1), :]) * features[span, :].astype(jnp.float32)).astype(mine.dtype)
    pl.semaphore_wait(barrier, len(partners))
    own = 2 * chip + core
    keep = pltpu.make_async_copy(mine, out.at[own], kept)
    keep.start()

    def chunk(q):
        return pl.ds(pl.multiple_of(q * part, part), part)

    def ring(direction, step, q, source, piece, target):
        return pltpu.make_async_remote_copy(
            src_ref=source,
            dst_ref=out.at[piece, chunk(q)],
            send_sem=ring_sent,
            recv_sem=ring_recv.at[(direction * half + step) * PARTS + q],
            device_id=target,
            device_id_type=MESH,
        )

    def side(direction, step, q, piece):
        return pltpu.make_async_remote_copy(
            src_ref=out.at[piece, chunk(q)],
            dst_ref=out.at[2 * chips + lax.rem(piece, 2 * half), chunk(q)],
            send_sem=side_sent,
            recv_sem=side_recv.at[(direction * half + step) * PARTS + q],
            device_id=side_to,
            device_id_type=MESH,
        )

    def share(source, piece, q):
        pltpu.make_async_remote_copy(
            src_ref=source,
            dst_ref=out.at[piece, chunk(q)],
            send_sem=mate_sent,
            recv_sem=mate_recv,
            device_id=mate,
            device_id_type=MESH,
        ).start()

    lengths = (half, half - 1)
    targets = (ahead, behind)

    def arrived(direction, step):
        c = around(-step if direction == 0 else step)
        return 2 * c + core, lax.div(c, half) != upper

    def tick(time, _):
        def each(q, _):
            step = time - SKEW * q

            @pl.when(step == 0)
            def _():
                source = mine.at[chunk(q)]
                ring(0, 0, q, source, own, ahead).start()
                ring(1, 0, q, source, own, behind).start()
                share(source, own, q)

            for direction in range(2):

                @pl.when((step >= 1) & (step <= lengths[direction]))
                def _():
                    piece, foreign = arrived(direction, step)
                    here = out.at[piece, chunk(q)]
                    ring(direction, step - 1, q, here, piece, targets[direction]).wait_recv()

                    @pl.when(step < lengths[direction])
                    def _():
                        ring(direction, step, q, here, piece, targets[direction]).start()

                    @pl.when(foreign)
                    def _():
                        side(direction, step - 1, q, piece).start()

                    share(here, piece, q)

            late = step - LAG
            for direction in range(2):

                @pl.when((late >= 1) & (late <= lengths[direction]))
                def _():
                    piece, foreign = arrived(direction, late)

                    @pl.when(foreign)
                    def _():
                        side(direction, late - 1, q, piece).wait_recv()
                        third = 2 * chips + lax.rem(piece, 2 * half)
                        share(out.at[third, chunk(q)], third, q)

            return 0

        return lax.fori_loop(0, PARTS, each, 0)

    lax.fori_loop(0, half + SKEW * (PARTS - 1) + LAG + 1, tick, 0)

    def drain(pieces, semaphore):
        span = out.at[pl.ds(0, pieces)]
        pltpu.make_async_copy(span, span, semaphore).wait()

    keep.wait()
    drain(chips - 1, ring_sent)
    drain(half, side_sent)
    drain(chips + half, mate_sent)
    drain(chips + half, mate_recv)


def farthest(t, size):
    step = lax.div(t + 1, 2)
    return size // 2 + jnp.where(lax.rem(t, 2) == 0, step, -step)


def layer_kernel(
    columns, half, tile_row, tile_col, tile_count, panels, edges, scale, weight, bias, cotangent,
    hidden, out, out_bias, total, summed, upstream, grad, grad_bias, from_mate, bias_mate, message, inbox, line, full,
    mate_recv, bias_recv, plane_recv, line_recv, back_recv, last_recv,
    mate_sent, bias_sent, plane_sent, line_sent, back_sent, last_sent,
):
    chips = 2 * half
    blk, rep, column, upper, chip, core = place(columns, half)
    mate = (blk, rep + 1 - 2 * core)
    x, y = lax.div(column, ACROSS), lax.rem(column, ACROSS)
    deep = columns // ACROSS
    lanes = out.shape[1] // TILE

    def each_plane(act):
        def body(e, _):
            to_x = lax.rem(x + farthest(lax.div(e, ACROSS), deep), deep)
            to_y = lax.rem(y + farthest(lax.rem(e, ACROSS), ACROSS), ACROSS)
            j = to_x * ACROSS + to_y
            act((2 * j + upper, rep), j)
            return 0

        lax.fori_loop(0, columns - 1, body, 0)

    def each_line(act):
        def body(e, _):
            c = lax.rem(chip + farthest(e, chips), chips)
            act((2 * column + lax.div(c, half), 2 * lax.rem(c, half) + core))
            return 0

        lax.fori_loop(0, chips - 1, body, 0)

    barrier = pltpu.get_barrier_semaphore()
    each_line(lambda device: pl.semaphore_signal(barrier, inc=1, device_id=device, device_id_type=MESH))
    each_plane(lambda device, j: pl.semaphore_signal(barrier, inc=1, device_id=device, device_id_type=MESH))
    pl.semaphore_signal(barrier, inc=1, device_id=mate, device_id_type=MESH)

    blks = lax.axis_size("blk")
    live = tile_count[0]
    tiles = total.shape[0]
    group_tiles = 2 * half * tiles
    total[...] = jnp.zeros_like(total)

    def multiply(b, _):
        products = []
        for i in range(BATCH):
            k = b * BATCH + i
            col = tile_col[0, k]
            offset = lax.rem(lax.div(col, group_tiles) - blk + blks, blks)
            part = jnp.where(offset == 0, upper, jnp.where(offset == jnp.where(upper == 0, 1, blks - 1), 1 - upper, 2))
            tile = part * group_tiles + lax.rem(col, group_tiles)
            products.append(jnp.dot(edges[k], panels[tile], preferred_element_type=jnp.float32))
        for t in range(tiles):
            added = total[t]
            for i in range(BATCH):
                k = b * BATCH + i
                added += jnp.where((tile_row[0, k] == t) & (k < live), 1.0, 0.0) * products[i]
            total[t] = added
        return 0

    lax.fori_loop(0, edges.shape[0] // BATCH, multiply, 0)
    for t in range(tiles):
        span = pl.ds(t * TILE, TILE)
        aggregated = (spread(scale[pl.ds(t, 1), :]) * total[t]).astype(jnp.bfloat16)
        summed[span, :] = aggregated
        preact = jnp.dot(aggregated, weight[...], preferred_element_type=jnp.float32) + bias[...]
        positive = preact > 0
        power = jnp.exp(jnp.minimum(preact, 0.0))
        hidden[span, :] = jnp.where(positive, preact, power - 1.0).astype(hidden.dtype)
        slope = jnp.where(positive, 1.0, power)
        upstream[span, :] = (cotangent[span, :].astype(jnp.float32) * slope).astype(upstream.dtype)
    weight_part = lax.dot_general(
        summed[...], upstream[...], (((0,), (0,)), ((), ())), preferred_element_type=jnp.float32
    )
    bias_part = jnp.sum(upstream[...].astype(jnp.float32), axis=0, keepdims=True)
    for c in range(2):
        for j in range(columns):
            r, s = divmod(c * columns + j, lanes)
            grad[c, j] = weight_part[8 * r : 8 * r + 8, TILE * s : TILE * (s + 1)]
    grad_bias[...] = jnp.zeros_like(grad_bias)
    for s in range(lanes):
        grad_bias[s : s + 1, :] = bias_part[:, TILE * s : TILE * (s + 1)]
    pl.semaphore_wait(barrier, columns + chips - 1)

    def remote(source, target, sent, received, device):
        return pltpu.make_async_remote_copy(
            src_ref=source, dst_ref=target, send_sem=sent, recv_sem=received, device_id=device, device_id_type=MESH
        )

    def landed(buffer, pieces, semaphore):
        span = buffer.at[pl.ds(0, pieces)]
        pltpu.make_async_copy(span, span, semaphore).wait()

    other = remote(grad.at[1 - core], from_mate, mate_sent, mate_recv, mate)
    other.start()
    other_bias = remote(grad_bias, bias_mate, bias_sent, bias_recv, mate)
    other_bias.start()
    other_bias.wait()
    bias_sum = grad_bias[...] + bias_mate[...]
    other.wait()
    for j in range(columns):
        message[j] = jnp.concatenate([grad[core, j] + from_mate[j], bias_sum], axis=0).astype(message.dtype)

    each_plane(lambda device, j: remote(message.at[j], inbox.at[column], plane_sent, plane_recv, device).start())
    inbox[column] = message[column]
    landed(inbox, columns - 1, plane_recv)
    line[chip] = jnp.sum(inbox[...].astype(jnp.float32), axis=0).astype(line.dtype)

    each_line(lambda device: remote(line.at[chip], line.at[chip], line_sent, line_recv, device).start())
    landed(line, chips - 1, line_recv)
    final = jnp.sum(line[...].astype(jnp.float32), axis=0)
    full[core, column] = final[0:8, :]
    out_bias[...] = final[8:16, :]

    here = full.at[core, column]
    each_plane(lambda device, j: remote(here, here, back_sent, back_recv, device).start())
    landed(full.at[core], columns - 1, back_recv)
    mine = full.at[core]
    last = remote(mine, mine, last_sent, last_recv, mate)
    last.start()
    last.wait()
    for c in range(2):
        for j in range(columns):
            r, s = divmod(c * columns + j, lanes)
            out[8 * r : 8 * r + 8, TILE * s : TILE * (s + 1)] = full[c, j]
    landed(message, columns - 1, plane_sent)
    landed(line, chips - 1, line_sent)
    landed(full.at[core], columns - 1, back_sent)


def shards(features, node_scale, weight, bias, cotangent, tile_row, tile_col, edge_weight, tile_count):
    rows, depth = features.shape
    width = weight.shape[1]
    columns = lax.axis_size("blk") // 2
    half = lax.axis_size("rep") // 2
    chips = 2 * half
    pieces = 2 * chips + 2 * half
    scale = node_scale.reshape(rows // TILE, TILE)
    vmem = pl.BlockSpec(memory_space=pltpu.VMEM)
    smem = pl.BlockSpec(memory_space=pltpu.SMEM)
    dma = pltpu.SemaphoreType.DMA

    gathered = pl.pallas_call(
        functools.partial(gather_kernel, columns, half),
        name="gather",
        out_shape=jax.ShapeDtypeStruct((pieces, rows, depth), jnp.bfloat16),
        in_specs=[vmem, vmem],
        out_specs=vmem,
        scratch_shapes=[
            pltpu.VMEM((rows, depth), jnp.bfloat16),
            dma((2 * half * PARTS,)),
            dma((2 * half * PARTS,)),
        ]
        + [dma(())] * 5,
        compiler_params=pltpu.CompilerParams(
            collective_id=0, has_side_effects=True, vmem_limit_bytes=VMEM_LIMIT
        ),
    )(features, scale)

    hidden, grad_weight, bias_sum = pl.pallas_call(
        functools.partial(layer_kernel, columns, half),
        name="layer",
        out_shape=(
            jax.ShapeDtypeStruct((rows, width), jnp.bfloat16),
            jax.ShapeDtypeStruct((depth, width), jnp.float32),
            jax.ShapeDtypeStruct((8, TILE), jnp.float32),
        ),
        in_specs=[smem] * 3 + [vmem] * 6,
        out_specs=(vmem, vmem, vmem),
        scratch_shapes=[
            pltpu.VMEM((rows // TILE, TILE, depth), jnp.float32),
            pltpu.VMEM((rows, depth), jnp.bfloat16),
            pltpu.VMEM((rows, width), jnp.bfloat16),
            pltpu.VMEM((2, columns, 8, TILE), jnp.float32),
            pltpu.VMEM((8, TILE), jnp.float32),
            pltpu.VMEM((columns, 8, TILE), jnp.float32),
            pltpu.VMEM((8, TILE), jnp.float32),
            pltpu.VMEM((columns, 16, TILE), WIRE),
            pltpu.VMEM((columns, 16, TILE), WIRE),
            pltpu.VMEM((chips, 16, TILE), WIRE),
            pltpu.VMEM((2, columns, 8, TILE), jnp.float32),
        ]
        + [dma(())] * 12,
        compiler_params=pltpu.CompilerParams(
            collective_id=1, has_side_effects=True, vmem_limit_bytes=VMEM_LIMIT
        ),
    )(
        tile_row, tile_col, tile_count, gathered.reshape(-1, TILE, depth), edge_weight[0], scale, weight,
        bias.reshape(1, width), cotangent,
    )
    return hidden, grad_weight, bias_sum.reshape(-1)[:width]


def solution(mesh):
    rows = P(("blk", "rep"))
    in_specs = (
        P(("blk", "rep"), None),
        rows,
        P(),
        P(),
        P(("blk", "rep"), None),
        P(("blk", "rep"), None),
        P(("blk", "rep"), None),
        P(("blk", "rep"), None, None, None),
        rows,
    )
    out_specs = (P(("blk", "rep"), None), P(), P())
    return jax.shard_map(shards, mesh=mesh, in_specs=in_specs, out_specs=out_specs, check_vma=False)
```
